32 devices in a mesh: slab: 2 (over x), row: 16 (over z, y, core).
Axes of the slice: x: 2, y: 2, z: 4, core: 2. Of those that a mesh axis runs over, the one named last changes fastest.
Arguments:
- sections: float32 [8, 512, 2048], P('slab', 'row'), parts along dimension 0, may hold values from -6 to 6
- valid: int32 [10, 16, 64], P('slab', 'row'), parts along dimension 0, may hold values 0 or 1
Outputs:
- flows: float32 [10, 2, 16, 64], P('slab', None, 'row'), parts along dimension 0
- displacement: float32 [8, 2, 16, 64], P('slab', None, 'row'), parts along dimension 0
The draws below stay inside these ranges and needn't reach their ends.
There are 2 independent parts, one for each index of `slab`. The reference program is written for one: setup_inputs(seed, part) draws one part's arguments, and reference() takes and returns one part's arrays. A program takes and returns all parts, laid end to end along the dimension named above; each array names one. Nothing has to cross between parts.
All inputs are finite; a program needn't handle non-finite values. No bound on the sum of `valid` on one device may be relied on, other than what follows from the above.
Results may differ from the reference program's by a relative error of at most 0.0001.
Values sent between devices are 32-bit elements; how exact they have to be, the bound alone decides.
A program may use at most 64 MiB of HBM per device.

```python
import jax
import jax.numpy as jnp

SECTIONS = 4
STRIDE = 32
PATCH = 64
RADIUS = 2
STEPS = 4
WIDTH = 2048
HEIGHT = 512
NODE_ROWS = 16
NODE_COLS = 64
NPAIRS = 5


def touch_ends(entries, key, low, largest):
    shape = entries.shape
    spot = [jax.random.randint(jax.random.fold_in(key, axis), (), 0, shape[axis]) for axis in range(len(shape))]
    entries = entries.at[tuple(spot)].set(low)
    longest = shape.index(max(shape))
    spot[longest] = (spot[longest] + 1) % shape[longest]
    return entries.at[tuple(spot)].set(largest)


def levels(stream_key, dims, cuts, least, largest):
    def one(dim, shards_of):
        steps = jax.random.uniform(jax.random.fold_in(jax.random.fold_in(stream_key, 6), dim), (shards_of,), jnp.float32, least / len(cuts), largest / len(cuts))
        return jnp.repeat(jnp.exp(steps), dims[dim] // shards_of).reshape((-1,) + (1,) * (len(dims) - dim - 1))

    loudness = one(*cuts[0])
    for cut in cuts[1:]:
        loudness = loudness * one(*cut)
    return loudness


def centred(rng, shape, deviation, most, cuts=(), held_as=jnp.bfloat16):
    entries = jax.random.normal(rng, shape, jnp.float32) * deviation
    if len(cuts) > 0:
        entries = levels(rng, shape, cuts, -0.22, 0.18) * entries
    return jnp.clip(entries, min=-most, max=most).astype(held_as)


def setup_inputs(seed: int = 0, part: int = 0) -> dict:
    keys = jax.random.split(jax.random.key(seed), 3)
    part_keys = jax.random.split(jax.random.fold_in(keys[2], part), 3)
    return {
        "sections": centred(part_keys[0], (SECTIONS, HEIGHT, WIDTH), 1.0, 6.0, ((1, 16),), jnp.float32),
        "valid": touch_ends((jax.random.randint(part_keys[1], (NPAIRS, NODE_ROWS, NODE_COLS), 0, 4) < 3).astype(jnp.int32), jax.random.fold_in(part_keys[1], 1), 0, 1),
    }


def pair_list():
    first = [(s, s + 1) for s in range(SECTIONS - 1)]
    second = [(s, s + 2) for s in range(SECTIONS - 2)]
    return first + second


def patch_columns(product):
    count = product.shape[0]
    halves = product.reshape(count, 2 * NODE_COLS, STRIDE // 2).sum(-1)
    padded = jnp.pad(halves, ((0, 0), (1, 1)))
    left = padded[:, :2 * NODE_COLS].reshape(count, NODE_COLS, 2).sum(-1)
    right = padded[:, 2:].reshape(count, NODE_COLS, 2).sum(-1)
    return left + right


def reference(sections, valid):
    margin = STRIDE // 2
    reach = RADIUS
    pairs = pair_list()
    offsets = jnp.arange(-reach, reach + 1).astype(jnp.float32)
    flow_list = []
    for first, second in pairs:
        fixed_img = jnp.pad(sections[first], ((margin, margin), (0, 0)))
        moving_img = jnp.pad(sections[second], ((margin + reach, margin + reach), (reach, reach)))
        corr_rows = []
        for shift_y in range(-reach, reach + 1):
            corr_cols = []
            for shift_x in range(-reach, reach + 1):
                moved = moving_img[reach + shift_y:reach + shift_y + HEIGHT + 2 * margin, reach + shift_x:reach + shift_x + WIDTH]
                columns = patch_columns(fixed_img * moved)
                padded = jnp.pad(columns, ((0, STRIDE - 2 * margin), (0, 0)))
                blocks = padded.reshape(NODE_ROWS + 1, STRIDE, NODE_COLS)
                total = blocks[:NODE_ROWS].sum(1) + blocks[1:, :2 * margin].sum(1)
                corr_cols.append(total / PATCH)
            corr_rows.append(jnp.stack(corr_cols))
        corr = jnp.stack(corr_rows)
        weight = corr * corr + 1.0
        denom = weight.sum((0, 1))
        flow_y = (offsets[:, None, None, None] * weight).sum((0, 1)) / denom
        flow_x = (offsets[None, :, None, None] * weight).sum((0, 1)) / denom
        flow_list.append(jnp.stack([flow_y, flow_x]))
    flows = jnp.stack(flow_list)
    masks = valid.astype(jnp.float32)
    pinned = (jnp.arange(SECTIONS) > 0).astype(jnp.float32)[:, None, None, None]
    moved_nodes = jnp.zeros((SECTIONS, 2, NODE_ROWS, NODE_COLS), jnp.float32)
    for turn_index in range(STEPS):
        padded = jnp.pad(moved_nodes, ((0, 0), (0, 0), (1, 1), (1, 1)))
        lap = 4.0 * moved_nodes - padded[:, :, :-2, 1:-1] - padded[:, :, 2:, 1:-1] - padded[:, :, 1:-1, :-2] - padded[:, :, 1:-1, 2:]
        grad = 1.0 * lap
        for index, (first, second) in enumerate(pairs):
            error = masks[index][None] * (moved_nodes[second] - moved_nodes[first] - flows[index])
            grad = grad.at[second].add(error).at[first].add(-error)
        moved_nodes = moved_nodes - 0.1 * grad * pinned
    return flows, moved_nodes
```

```python
import functools

import jax
import jax.numpy as jnp
from jax import lax
from jax.experimental import pallas as pl
from jax.experimental.pallas import tpu as pltpu
from jax.sharding import PartitionSpec as P

PATCH = 64
RADIUS = 2
STEPS = 4
LANES = 128
SPAN = STEPS - 1
PAIRS = ((0, 1), (1, 2), (2, 3), (0, 2), (1, 3))
SHIFTS = 2 * RADIUS + 1
TERMS = len(PAIRS) * SHIFTS
BF16 = jnp.bfloat16
F32 = jnp.float32


def thirds(value):
    high = value.astype(BF16)
    rest = value - high.astype(F32)
    middle = rest.astype(BF16)
    low = (rest - middle.astype(F32)).astype(BF16)
    return high, middle, low


def exact_dot(value, ones):
    return sum(jnp.dot(part, ones, preferred_element_type=F32) for part in thirds(value))


def shifted(row, shift):
    if shift == 0:
        return row
    blocks = row.shape[0]
    lane = lax.broadcasted_iota(jnp.int32, row.shape, 1)
    block = lax.broadcasted_iota(jnp.int32, row.shape, 0)
    if shift > 0:
        other = jnp.where(block == blocks - 1, 0.0, pltpu.roll(row, blocks - 1, 0))
        return pltpu.roll(jnp.where(lane < shift, other, row), LANES - shift, 1)
    other = jnp.where(block == 0, 0.0, pltpu.roll(row, 1, 0))
    return pltpu.roll(jnp.where(lane >= LANES + shift, other, row), -shift, 1)


def kernel(
    rows_of, sections, valid, flows_out, moved_out,
    natural, image, moving, halo, halo_moving, sums, ones, reduced, arrived, notes,
    load_sem, halo_send, halo_recv, band_send, band_recv, note_send, note_recv,
):
    me = lax.axis_index("row")
    count, stride, width = natural.shape
    blocks = width // LANES
    halves = blocks // 8
    band = stride // 2
    node_cols = width // stride

    loads = [
        pltpu.make_async_copy(sections.at[s], natural.at[s], load_sem.at[s])
        for s in range(count)
    ]
    for load in loads:
        load.start()

    halo[...] = jnp.zeros(halo.shape, F32)
    arrived[...] = jnp.zeros(arrived.shape, F32)
    notes[...] = jnp.zeros(notes.shape, F32)
    barrier = pltpu.get_barrier_semaphore()
    offsets = [o for k in range(1, SPAN + 1) for o in (-k, k)]

    def inside(offset):
        return me >= -offset if offset < 0 else me < rows_of - offset

    for offset in offsets:
        @pl.when(inside(offset))
        def _():
            pl.semaphore_signal(
                barrier, inc=1, device_id={"row": me + offset},
                device_id_type=pl.DeviceIdType.MESH,
            )

    for b in range(2):
        for half in range(halves):
            sums[b, half, TERMS * SHIFTS * 8:, :] = jnp.zeros(
                (sums.shape[2] - TERMS * SHIFTS * 8, LANES), F32
            )
    for t in range(blocks):
        column = lax.broadcasted_iota(jnp.int32, (LANES, LANES), 0) + t * LANES
        lane = lax.broadcasted_iota(jnp.int32, (LANES, LANES), 1)
        node = jnp.where(lane < node_cols, lane, lane - node_cols)
        first = node * stride - stride // 2
        hit = (column >= first) & (column < first + PATCH)
        ones[t * LANES:(t + 1) * LANES, :] = jnp.where(hit, 1.0, 0.0).astype(BF16)

    for s in range(count):
        loads[s].wait()

        @pl.loop(0, stride // 8)
        def _(tile):
            base = pl.multiple_of((s * stride + tile * 8) * blocks, 8)
            top = pl.multiple_of(tile * 8, 8)
            for t in range(blocks):
                image[pl.ds(base + t, 8, stride=blocks), :] = natural[
                    s, pl.ds(top, 8), t * LANES:(t + 1) * LANES
                ]

    size = RADIUS * blocks
    signals = jnp.minimum(me, SPAN) + jnp.minimum(rows_of - 1 - me, SPAN)
    pl.semaphore_wait(barrier, signals)

    def halo_copy(side, s):
        row = 0 if side == 0 else stride - RADIUS
        start = (s * stride + row) * blocks
        return pltpu.make_async_remote_copy(
            src_ref=image.at[pl.ds(start, size)],
            dst_ref=halo.at[1 - side, s - 1],
            send_sem=halo_send.at[side, s - 1],
            recv_sem=halo_recv.at[1 - side, s - 1],
            device_id={"row": me - 1 if side == 0 else me + 1},
            device_id_type=pl.DeviceIdType.MESH,
        )

    def on_side(side):
        return pl.when(inside(-1 if side == 0 else 1))

    for side in range(2):
        @on_side(side)
        def _():
            for s in range(1, count):
                halo_copy(side, s).start()

    @pl.loop(0, stride)
    def _(row):
        for s in range(1, count):
            start = pl.multiple_of((s * stride + row) * blocks, 8)
            value = image[pl.ds(start, blocks), :]
            for x in range(SHIFTS):
                moving[x, s - 1, row] = shifted(value, x - RADIUS)

    @pl.loop(0, SHIFTS * halves)
    def _(turn):
        x = turn // halves
        half = turn % halves
        sub = pl.multiple_of(half * 8, 8)
        out = pl.multiple_of(x * (TERMS * 8), 8)
        for b in range(2):
            totals = [None] * TERMS
            for y in range(b * band, (b + 1) * band):
                fixed = [
                    image[pl.ds(pl.multiple_of((s * stride + y) * blocks + sub, 8), 8), :]
                    for s in range(count - 1)
                ]
                for v in range(SHIFTS):
                    other = y + v - RADIUS
                    if other < 0 or other >= stride:
                        continue
                    moved = [moving[x, s, other, pl.ds(sub, 8), :] for s in range(count - 1)]
                    for p, (first, second) in enumerate(PAIRS):
                        product = fixed[first] * moved[second - 1]
                        i = p * SHIFTS + v
                        totals[i] = product if totals[i] is None else totals[i] + product
            for i in range(TERMS):
                sums[b, half, pl.ds(pl.multiple_of(out + i * 8, 8), 8), :] = totals[i]

    for side in range(2):
        @on_side(side)
        def _():
            for s in range(1, count):
                pltpu.make_async_copy(
                    halo.at[side, s - 1], halo.at[side, s - 1], halo_recv.at[side, s - 1]
                ).wait()

    for side in range(2):
        @pl.loop(0, RADIUS)
        def _(row):
            for s in range(count - 1):
                value = halo[side, s, pl.ds(pl.multiple_of(row * blocks, 8), blocks), :]
                for x in range(SHIFTS):
                    halo_moving[x, side, s, row] = shifted(value, x - RADIUS)

    @pl.loop(0, SHIFTS * halves)
    def _(turn):
        x = turn // halves
        half = turn % halves
        sub = pl.multiple_of(half * 8, 8)
        out = pl.multiple_of(x * (TERMS * 8), 8)
        for b in range(2):
            totals = {}
            for y in range(b * band, (b + 1) * band):
                for v in range(SHIFTS):
                    other = y + v - RADIUS
                    if 0 <= other < stride:
                        continue
                    row = other + RADIUS if other < 0 else other - stride
                    for p, (first, second) in enumerate(PAIRS):
                        at = pl.multiple_of((first * stride + y) * blocks + sub, 8)
                        product = image[pl.ds(at, 8), :] * halo_moving[
                            x, b, second - 1, row, pl.ds(sub, 8), :
                        ]
                        i = p * SHIFTS + v
                        totals[i] = totals[i] + product if i in totals else product
            for i, total in totals.items():
                at = pl.ds(pl.multiple_of(out + i * 8, 8), 8)
                sums[b, half, at, :] = sums[b, half, at, :] + total

    def band_copy(side):
        return pltpu.make_async_remote_copy(
            src_ref=reduced.at[side],
            dst_ref=arrived.at[1 - side],
            send_sem=band_send.at[side],
            recv_sem=band_recv.at[1 - side],
            device_id={"row": me - 1 if side == 0 else me + 1},
            device_id_type=pl.DeviceIdType.MESH,
        )

    for b in range(2):
        total = jnp.zeros((LANES, LANES), F32)
        for t in range(0, blocks, 2):
            wide = jnp.concatenate(
                [sums[b, k // 8, pl.ds(k % 8, LANES, stride=8), :] for k in (t, t + 1)], axis=1
            )
            total = total + exact_dot(wide, ones[t * LANES:(t + 2) * LANES, :])
        reduced[b] = total

        @on_side(b)
        def _():
            band_copy(b).start()

    term = lax.broadcasted_iota(jnp.int32, (32, LANES), 1)
    line = lax.broadcasted_iota(jnp.int32, (32, LANES), 0)
    shift_x = sum((term >= TERMS * k).astype(jnp.int32) for k in range(1, SHIFTS))
    rest = term - TERMS * shift_x
    pair = sum((rest >= SHIFTS * k).astype(jnp.int32) for k in range(1, len(PAIRS)))
    shift_y = rest - SHIFTS * pair
    kind = (line >= 8).astype(jnp.int32) + (line >= 16).astype(jnp.int32)
    factor = jnp.where(kind == 0, 1, jnp.where(kind == 1, shift_y - RADIUS, shift_x - RADIUS))
    belongs = (pair == line - 8 * kind) & (term < TERMS * SHIFTS) & (line < 24)
    weights_of = jnp.where(belongs, factor, 0).astype(F32).astype(BF16)

    for side in range(2):
        @on_side(side)
        def _():
            pltpu.make_async_copy(
                arrived.at[side], arrived.at[side], band_recv.at[side]
            ).wait()

    corr = (reduced[0] + reduced[1] + arrived[0] + arrived[1]) * (1.0 / PATCH)
    weight = corr * corr + 1.0
    moments = sum(
        jnp.dot(weights_of, part, preferred_element_type=F32) for part in thirds(weight)
    )
    lane = lax.broadcasted_iota(jnp.int32, (8, LANES), 1)
    line = lax.broadcasted_iota(jnp.int32, (8, LANES), 0)
    npairs = len(PAIRS)
    denom = jnp.where(line < npairs, moments[0:8], 1.0)
    flow = jnp.where(lane < node_cols, moments[8:16], moments[16:24]) / denom
    mask = valid[:, 0, :].astype(F32)
    notes[SPAN, 0:8, :] = flow
    notes[SPAN, 8:8 + npairs, 0:node_cols] = mask
    notes[SPAN, 8:8 + npairs, node_cols:2 * node_cols] = mask

    def note_copy(k):
        offset = offsets[k]
        return pltpu.make_async_remote_copy(
            src_ref=notes.at[SPAN],
            dst_ref=notes.at[SPAN - offset],
            send_sem=note_send.at[k],
            recv_sem=note_recv.at[SPAN - offset],
            device_id={"row": me + offset},
            device_id_type=pl.DeviceIdType.MESH,
        )

    for k, offset in enumerate(offsets):
        @pl.when(inside(offset))
        def _():
            note_copy(k).start()

    flows_out[:, 0, 0, :] = flow[:npairs, :node_cols]
    flows_out[:, 1, 0, :] = flow[:npairs, node_cols:]

    for k, offset in enumerate(offsets):
        @pl.when(inside(offset))
        def _():
            slot = SPAN + offset
            pltpu.make_async_copy(notes.at[slot], notes.at[slot], note_recv.at[slot]).wait()

    node_row = me - SPAN + line
    keep = jnp.where((node_row >= 0) & (node_row < rows_of), 0.1, 0.0)
    at_left = (lane == 0) | (lane == node_cols)
    at_right = (lane == node_cols - 1) | (lane == 2 * node_cols - 1)
    flow_rows = [notes[:, p, :] for p in range(npairs)]
    mask_rows = [notes[:, 8 + p, :] for p in range(npairs)]
    moved = [jnp.zeros((8, LANES), F32) for _ in range(count)]
    for step in range(STEPS):
        grad = [None] * count
        for s in range(1, count):
            d = moved[s]
            left = jnp.where(at_left, 0.0, pltpu.roll(d, 1, 1))
            right = jnp.where(at_right, 0.0, pltpu.roll(d, LANES - 1, 1))
            grad[s] = 4.0 * d - pltpu.roll(d, 1, 0) - pltpu.roll(d, 7, 0) - left - right
        for p, (first, second) in enumerate(PAIRS):
            error = mask_rows[p] * (moved[second] - moved[first] - flow_rows[p])
            grad[second] = grad[second] + error
            if first > 0:
                grad[first] = grad[first] - error
        moved = [moved[0]] + [moved[s] - keep * grad[s] for s in range(1, count)]
    for s in range(count):
        moved_out[s, 0] = moved[s][SPAN:SPAN + 1, :node_cols]
        moved_out[s, 1] = moved[s][SPAN:SPAN + 1, node_cols:]

    for side in range(2):
        @on_side(side)
        def _():
            for s in range(1, count):
                halo_copy(side, s).wait_send()
            band_copy(side).wait_send()
    for k, offset in enumerate(offsets):
        @pl.when(inside(offset))
        def _():
            note_copy(k).wait_send()


def local(rows_of, sections, valid):
    count, stride, width = sections.shape
    blocks = width // LANES
    npairs = valid.shape[0]
    node_cols = width // stride
    moving = count - 1
    terms = TERMS * SHIFTS
    return pl.pallas_call(
        functools.partial(kernel, rows_of),
        out_shape=(
            jax.ShapeDtypeStruct((npairs, 2, 1, node_cols), F32),
            jax.ShapeDtypeStruct((count, 2, 1, node_cols), F32),
        ),
        in_specs=[
            pl.BlockSpec(memory_space=pl.ANY),
            pl.BlockSpec(memory_space=pltpu.VMEM),
        ],
        out_specs=(
            pl.BlockSpec(memory_space=pltpu.VMEM),
            pl.BlockSpec(memory_space=pltpu.VMEM),
        ),
        scratch_shapes=[
            pltpu.VMEM((count, stride, width), F32),
            pltpu.VMEM((count * stride * blocks, LANES), F32),
            pltpu.VMEM((SHIFTS, moving, stride, blocks, LANES), F32),
            pltpu.VMEM((2, moving, RADIUS * blocks, LANES), F32),
            pltpu.VMEM((SHIFTS, 2, moving, RADIUS, blocks, LANES), F32),
            pltpu.VMEM((2, blocks // 8, -(-terms // 8) * 64, LANES), F32),
            pltpu.VMEM((width, LANES), BF16),
            pltpu.VMEM((2, LANES, LANES), F32),
            pltpu.VMEM((2, LANES, LANES), F32),
            pltpu.VMEM((8, 16, LANES), F32),
            pltpu.SemaphoreType.DMA((count,)),
            pltpu.SemaphoreType.DMA((2, moving)),
            pltpu.SemaphoreType.DMA((2, moving)),
            pltpu.SemaphoreType.DMA((2,)),
            pltpu.SemaphoreType.DMA((2,)),
            pltpu.SemaphoreType.DMA((2 * SPAN,)),
            pltpu.SemaphoreType.DMA((2 * SPAN + 1,)),
        ],
        compiler_params=pltpu.CompilerParams(
            collective_id=0, has_side_effects=True, vmem_limit_bytes=32 * 2**20
        ),
    )(sections, valid)


def solution(mesh):
    return jax.shard_map(
        functools.partial(local, mesh.shape["row"]),
        mesh=mesh,
        in_specs=(P("slab", "row", None), P("slab", "row", None)),
        out_specs=(P("slab", None, "row", None), P("slab", None, "row", None)),
        check_vma=False,
    )
```

```python
import functools

import jax
import jax.numpy as jnp
from jax import lax
from jax.experimental import pallas as pl
from jax.experimental.pallas import tpu as pltpu
from jax.sharding import PartitionSpec as P

PATCH = 64
RADIUS = 2
STEPS = 4
LANES = 128
SPAN = STEPS - 1
PAIRS = ((0, 1), (1, 2), (2, 3), (0, 2), (1, 3))
SHIFTS = 2 * RADIUS + 1
TERMS = len(PAIRS) * SHIFTS
BF16 = jnp.bfloat16
F32 = jnp.float32


def thirds(value):
    high = value.astype(BF16)
    rest = value - high.astype(F32)
    middle = rest.astype(BF16)
    low = (rest - middle.astype(F32)).astype(BF16)
    return high, middle, low


def exact_dot(value, ones):
    rows = value.shape[0]
    parts = jnp.dot(
        jnp.concatenate(thirds(value), axis=0), ones, preferred_element_type=F32
    )
    return parts[:rows] + parts[rows:2 * rows] + parts[2 * rows:]


def shifted(row, shift):
    if shift == 0:
        return row
    blocks = row.shape[0]
    lane = lax.broadcasted_iota(jnp.int32, row.shape, 1)
    block = lax.broadcasted_iota(jnp.int32, row.shape, 0)
    if shift > 0:
        other = jnp.where(block == blocks - 1, 0.0, pltpu.roll(row, blocks - 1, 0))
        return pltpu.roll(jnp.where(lane < shift, other, row), LANES - shift, 1)
    other = jnp.where(block == 0, 0.0, pltpu.roll(row, 1, 0))
    return pltpu.roll(jnp.where(lane >= LANES + shift, other, row), -shift, 1)


def kernel(
    rows_of, sections, valid, rows_out,
    natural, image, moving, halo, halo_moving, sums, ones, reduced, arrived, notes,
    load_sem, halo_send, halo_recv, band_send, band_recv, note_send, note_recv, mask_in, mask_notes, mask_load, mask_send, mask_recv,
):
    me = lax.axis_index("row")
    count, stride, width = natural.shape
    blocks = width // LANES
    halves = blocks // 8
    band = stride // 2
    node_cols = width // stride

    loads = [
        pltpu.make_async_copy(sections.at[s], natural.at[s], load_sem.at[s])
        for s in range(count)
    ]
    for load in loads:
        load.start()

    mask_copy_in = pltpu.make_async_copy(valid, mask_in, mask_load)
    mask_copy_in.start()

    halo[...] = jnp.zeros(halo.shape, F32)
    arrived[...] = jnp.zeros(arrived.shape, F32)
    notes[...] = jnp.zeros(notes.shape, F32)
    mask_notes[...] = jnp.zeros(mask_notes.shape, F32)
    barrier = pltpu.get_barrier_semaphore()
    offsets = [o for k in range(1, SPAN + 1) for o in (-k, k)]

    def inside(offset):
        return me >= -offset if offset < 0 else me < rows_of - offset

    for offset in offsets:
        @pl.when(inside(offset))
        def _():
            pl.semaphore_signal(
                barrier, inc=1, device_id={"row": me + offset},
                device_id_type=pl.DeviceIdType.MESH,
            )

    for b in range(2):
        for half in range(halves):
            sums[b, half, TERMS * SHIFTS * 8:, :] = jnp.zeros(
                (sums.shape[2] - TERMS * SHIFTS * 8, LANES), F32
            )
    for t in range(blocks):
        column = lax.broadcasted_iota(jnp.int32, (LANES, LANES), 0) + t * LANES
        lane = lax.broadcasted_iota(jnp.int32, (LANES, LANES), 1)
        node = jnp.where(lane < node_cols, lane, lane - node_cols)
        first = node * stride - stride // 2
        hit = (column >= first) & (column < first + PATCH)
        ones[t * LANES:(t + 1) * LANES, :] = jnp.where(hit, 1.0, 0.0).astype(BF16)

    for s in range(count):
        loads[s].wait()

        @pl.loop(0, stride // 8)
        def _(tile):
            base = pl.multiple_of(tile * 8 * blocks, 8)
            top = pl.multiple_of(tile * 8, 8)
            for t in range(blocks):
                image[s, pl.ds(base + t, 8, stride=blocks), :] = natural[
                    s, pl.ds(top, 8), t * LANES:(t + 1) * LANES
                ]

    size = RADIUS * blocks
    signals = jnp.minimum(me, SPAN) + jnp.minimum(rows_of - 1 - me, SPAN)
    pl.semaphore_wait(barrier, signals)

    def halo_copy(side):
        row = 0 if side == 0 else stride - RADIUS
        start = row * blocks
        return pltpu.make_async_remote_copy(
            src_ref=image.at[1:count, pl.ds(start, size)],
            dst_ref=halo.at[1 - side],
            send_sem=halo_send.at[side],
            recv_sem=halo_recv.at[1 - side],
            device_id={"row": me - 1 if side == 0 else me + 1},
            device_id_type=pl.DeviceIdType.MESH,
        )

    def on_side(side):
        return pl.when(inside(-1 if side == 0 else 1))

    for side in range(2):
        @on_side(side)
        def _():
            halo_copy(side).start()

    npairs = len(PAIRS)

    def row_copy(k, rows, sends, recvs):
        offset = offsets[k]
        return pltpu.make_async_remote_copy(
            src_ref=rows.at[SPAN],
            dst_ref=rows.at[SPAN - offset],
            send_sem=sends.at[k],
            recv_sem=recvs.at[SPAN - offset],
            device_id={"row": me + offset},
            device_id_type=pl.DeviceIdType.MESH,
        )

    mask_copy_in.wait()
    mask = mask_in[:, 0, :].astype(F32)
    mask_notes[SPAN, 0:npairs, 0:node_cols] = mask
    mask_notes[SPAN, 0:npairs, node_cols:2 * node_cols] = mask
    for k, offset in enumerate(offsets):
        @pl.when(inside(offset))
        def _():
            row_copy(k, mask_notes, mask_send, mask_recv).start()

    @pl.loop(0, stride, unroll=8)
    def _(row):
        for s in range(1, count):
            start = pl.multiple_of(row * blocks, 8)
            value = image[s, pl.ds(start, blocks), :]
            for x in range(SHIFTS):
                moving[x, s - 1, row] = shifted(value, x - RADIUS)

    @pl.loop(0, SHIFTS * halves)
    def _(turn):
        x = turn // halves
        half = turn % halves
        sub = pl.multiple_of(half * 8, 8)
        out = pl.multiple_of(x * (TERMS * 8), 8)
        for b in range(2):
            totals = [None] * TERMS
            for y in range(b * band, (b + 1) * band):
                fixed = [
                    image[s, pl.ds(pl.multiple_of(y * blocks + sub, 8), 8), :]
                    for s in range(count - 1)
                ]
                for v in range(SHIFTS):
                    other = y + v - RADIUS
                    if other < 0 or other >= stride:
                        continue
                    moved = [moving[x, s, other, pl.ds(sub, 8), :] for s in range(count - 1)]
                    for p, (first, second) in enumerate(PAIRS):
                        product = fixed[first] * moved[second - 1]
                        i = p * SHIFTS + v
                        totals[i] = product if totals[i] is None else totals[i] + product
            for i in range(TERMS):
                sums[b, half, pl.ds(pl.multiple_of(out + i * 8, 8), 8), :] = totals[i]

    for side in range(2):
        @on_side(side)
        def _():
            pltpu.make_async_copy(halo.at[side], halo.at[side], halo_recv.at[side]).wait()

    for side in range(2):
        @pl.loop(0, RADIUS, unroll=2)
        def _(row):
            for s in range(count - 1):
                value = halo[side, s, pl.ds(pl.multiple_of(row * blocks, 8), blocks), :]
                for x in range(SHIFTS):
                    halo_moving[x, side, s, row] = shifted(value, x - RADIUS)

    @pl.loop(0, SHIFTS * halves)
    def _(turn):
        x = turn // halves
        half = turn % halves
        sub = pl.multiple_of(half * 8, 8)
        out = pl.multiple_of(x * (TERMS * 8), 8)
        for b in range(2):
            totals = {}
            for y in range(b * band, (b + 1) * band):
                for v in range(SHIFTS):
                    other = y + v - RADIUS
                    if 0 <= other < stride:
                        continue
                    row = other + RADIUS if other < 0 else other - stride
                    for p, (first, second) in enumerate(PAIRS):
                        at = pl.multiple_of(y * blocks + sub, 8)
                        product = image[first, pl.ds(at, 8), :] * halo_moving[
                            x, b, second - 1, row, pl.ds(sub, 8), :
                        ]
                        i = p * SHIFTS + v
                        totals[i] = totals[i] + product if i in totals else product
            for i, total in totals.items():
                at = pl.ds(pl.multiple_of(out + i * 8, 8), 8)
                sums[b, half, at, :] = sums[b, half, at, :] + total

    def band_copy(side):
        return pltpu.make_async_remote_copy(
            src_ref=reduced.at[side],
            dst_ref=arrived.at[1 - side],
            send_sem=band_send.at[side],
            recv_sem=band_recv.at[1 - side],
            device_id={"row": me - 1 if side == 0 else me + 1},
            device_id_type=pl.DeviceIdType.MESH,
        )

    first_half = lax.broadcasted_iota(jnp.int32, (LANES // 2, LANES), 1) < node_cols
    for b in range(2):
        total = jnp.zeros((LANES, LANES), F32)
        for t in range(0, blocks, 2):
            wide = jnp.concatenate(
                [sums[b, k // 8, pl.ds(k % 8, LANES, stride=8), :] for k in (t, t + 1)], axis=1
            )
            total = total + exact_dot(wide, ones[t * LANES:(t + 2) * LANES, :])
        reduced[b] = jnp.where(first_half, total[:LANES // 2], total[LANES // 2:])

        @on_side(b)
        def _():
            band_copy(b).start()

    term = lax.broadcasted_iota(jnp.int32, (32, LANES), 1)
    line = lax.broadcasted_iota(jnp.int32, (32, LANES), 0)
    shift_x = sum((term >= TERMS * k).astype(jnp.int32) for k in range(1, SHIFTS))
    rest = term - TERMS * shift_x
    pair = sum((rest >= SHIFTS * k).astype(jnp.int32) for k in range(1, len(PAIRS)))
    shift_y = rest - SHIFTS * pair
    kind = (line >= 8).astype(jnp.int32) + (line >= 16).astype(jnp.int32)
    factor = jnp.where(kind == 0, 1, jnp.where(kind == 1, shift_y - RADIUS, shift_x - RADIUS))
    belongs = (pair == line - 8 * kind) & (term < TERMS * SHIFTS) & (line < 24)
    weights_of = jnp.where(belongs, factor, 0).astype(F32).astype(BF16)

    for side in range(2):
        @on_side(side)
        def _():
            pltpu.make_async_copy(
                arrived.at[side], arrived.at[side], band_recv.at[side]
            ).wait()

    corr = (reduced[0] + reduced[1] + arrived[0] + arrived[1]) * (1.0 / PATCH)
    weight = corr * corr + 1.0
    parts = thirds(weight)
    low, high = (
        sum(jnp.dot(half, part, preferred_element_type=F32) for part in parts)
        for half in (weights_of[:, :LANES // 2], weights_of[:, LANES // 2:])
    )
    moments = jnp.where(
        lax.broadcasted_iota(jnp.int32, low.shape, 1) < node_cols, low, high
    )
    moments = moments + pltpu.roll(moments, LANES // 2, 1)
    lane = lax.broadcasted_iota(jnp.int32, (8, LANES), 1)
    line = lax.broadcasted_iota(jnp.int32, (8, LANES), 0)
    denom = jnp.where(line < npairs, moments[0:8], 1.0)
    flow = jnp.where(lane < node_cols, moments[8:16], moments[16:24]) / denom
    notes[SPAN] = flow

    for k, offset in enumerate(offsets):
        @pl.when(inside(offset))
        def _():
            row_copy(k, notes, note_send, note_recv).start()

    for k, offset in enumerate(offsets):
        @pl.when(inside(offset))
        def _():
            slot = SPAN + offset
            pltpu.make_async_copy(
                mask_notes.at[slot], mask_notes.at[slot], mask_recv.at[slot]
            ).wait()
            pltpu.make_async_copy(notes.at[slot], notes.at[slot], note_recv.at[slot]).wait()

    rows_out[0] = notes[...]
    rows_out[1] = mask_notes[...]

    for side in range(2):
        @on_side(side)
        def _():
            halo_copy(side).wait_send()
            band_copy(side).wait_send()
    for k, offset in enumerate(offsets):
        @pl.when(inside(offset))
        def _():
            row_copy(k, mask_notes, mask_send, mask_recv).wait_send()
            row_copy(k, notes, note_send, note_recv).wait_send()


def relax_kernel(rows_of, rows, flows_out, moved_out):
    me = lax.axis_index("row")
    npairs, _, _, node_cols = flows_out.shape
    count = moved_out.shape[0]
    lane = lax.broadcasted_iota(jnp.int32, (8, LANES), 1)
    line = lax.broadcasted_iota(jnp.int32, (8, LANES), 0)
    flow = rows[0, SPAN]
    flows_out[:, 0, 0, :] = flow[:npairs, :node_cols]
    flows_out[:, 1, 0, :] = flow[:npairs, node_cols:]
    node_row = me - SPAN + line
    keep = jnp.where((node_row >= 0) & (node_row < rows_of), 0.1, 0.0)
    at_left = (lane == 0) | (lane == node_cols)
    at_right = (lane == node_cols - 1) | (lane == 2 * node_cols - 1)
    flow_rows = [rows[0, :, p, :] for p in range(npairs)]
    mask_rows = [rows[1, :, p, :] for p in range(npairs)]
    moved = [jnp.zeros((8, LANES), F32) for _ in range(count)]
    for step in range(STEPS):
        grad = [None] * count
        for s in range(1, count):
            d = moved[s]
            left = jnp.where(at_left, 0.0, pltpu.roll(d, 1, 1))
            right = jnp.where(at_right, 0.0, pltpu.roll(d, LANES - 1, 1))
            grad[s] = 4.0 * d - pltpu.roll(d, 1, 0) - pltpu.roll(d, 7, 0) - left - right
        for p, (first, second) in enumerate(PAIRS):
            error = mask_rows[p] * (moved[second] - moved[first] - flow_rows[p])
            grad[second] = grad[second] + error
            if first > 0:
                grad[first] = grad[first] - error
        moved = [moved[0]] + [moved[s] - keep * grad[s] for s in range(1, count)]
    for s in range(count):
        moved_out[s, 0] = moved[s][SPAN:SPAN + 1, :node_cols]
        moved_out[s, 1] = moved[s][SPAN:SPAN + 1, node_cols:]


def local(rows_of, sections, valid):
    count, stride, width = sections.shape
    blocks = width // LANES
    npairs = valid.shape[0]
    node_cols = width // stride
    moving = count - 1
    terms = TERMS * SHIFTS
    rows = pl.pallas_call(
        functools.partial(kernel, rows_of),
        out_shape=jax.ShapeDtypeStruct((2, 8, 8, LANES), F32),
        in_specs=[
            pl.BlockSpec(memory_space=pl.ANY),
            pl.BlockSpec(memory_space=pl.ANY),
        ],
        out_specs=pl.BlockSpec(memory_space=pltpu.VMEM),
        scratch_shapes=[
            pltpu.VMEM((count, stride, width), F32),
            pltpu.VMEM((count, stride * blocks, LANES), F32),
            pltpu.VMEM((SHIFTS, moving, stride, blocks, LANES), F32),
            pltpu.VMEM((2, moving, RADIUS * blocks, LANES), F32),
            pltpu.VMEM((SHIFTS, 2, moving, RADIUS, blocks, LANES), F32),
            pltpu.VMEM((2, blocks // 8, -(-terms // 8) * 64, LANES), F32),
            pltpu.VMEM((width, LANES), BF16),
            pltpu.VMEM((2, LANES // 2, LANES), F32),
            pltpu.VMEM((2, LANES // 2, LANES), F32),
            pltpu.VMEM((8, 8, LANES), F32),
            pltpu.SemaphoreType.DMA((count,)),
            pltpu.SemaphoreType.DMA((2,)),
            pltpu.SemaphoreType.DMA((2,)),
            pltpu.SemaphoreType.DMA((2,)),
            pltpu.SemaphoreType.DMA((2,)),
            pltpu.SemaphoreType.DMA((2 * SPAN,)),
            pltpu.SemaphoreType.DMA((2 * SPAN + 1,)),
            pltpu.VMEM(valid.shape, jnp.int32),
            pltpu.VMEM((8, 8, LANES), F32),
            pltpu.SemaphoreType.DMA,
            pltpu.SemaphoreType.DMA((2 * SPAN,)),
            pltpu.SemaphoreType.DMA((2 * SPAN + 1,)),
        ],
        compiler_params=pltpu.CompilerParams(
            collective_id=0, has_side_effects=True, vmem_limit_bytes=60 * 2**20
        ),
    )(sections, valid)
    return pl.pallas_call(
        functools.partial(relax_kernel, rows_of),
        out_shape=(
            jax.ShapeDtypeStruct((npairs, 2, 1, node_cols), F32),
            jax.ShapeDtypeStruct((count, 2, 1, node_cols), F32),
        ),
        in_specs=[pl.BlockSpec(memory_space=pltpu.VMEM)],
        out_specs=(
            pl.BlockSpec(memory_space=pltpu.VMEM),
            pl.BlockSpec(memory_space=pltpu.VMEM),
        ),
    )(rows)


def solution(mesh):
    return jax.shard_map(
        functools.partial(local, mesh.shape["row"]),
        mesh=mesh,
        in_specs=(P("slab", "row", None), P("slab", "row", None)),
        out_specs=(P("slab", None, "row", None), P("slab", None, "row", None)),
        check_vma=False,
    )
```

```python
import functools

import jax
import jax.numpy as jnp
from jax import lax
from jax.experimental import pallas as pl
from jax.experimental.pallas import tpu as pltpu
from jax.sharding import PartitionSpec as P

PATCH = 64
RADIUS = 2
STEPS = 4
LANES = 128
SPAN = STEPS - 1
PAIRS = ((0, 1), (1, 2), (2, 3), (0, 2), (1, 3))
SHIFTS = 2 * RADIUS + 1
TERMS = len(PAIRS) * SHIFTS
BF16 = jnp.bfloat16
F32 = jnp.float32


def thirds(value):
    high = value.astype(BF16)
    rest = value - high.astype(F32)
    middle = rest.astype(BF16)
    low = (rest - middle.astype(F32)).astype(BF16)
    return high, middle, low


def shifted(row, shift):
    if shift == 0:
        return row
    blocks = row.shape[0]
    lane = lax.broadcasted_iota(jnp.int32, row.shape, 1)
    block = lax.broadcasted_iota(jnp.int32, row.shape, 0)
    if shift > 0:
        other = jnp.where(block == blocks - 1, 0.0, pltpu.roll(row, blocks - 1, 0))
        return pltpu.roll(jnp.where(lane < shift, other, row), LANES - shift, 1)
    other = jnp.where(block == 0, 0.0, pltpu.roll(row, 1, 0))
    return pltpu.roll(jnp.where(lane >= LANES + shift, other, row), -shift, 1)


def kernel(
    rows_of, sections, valid, rows_out,
    natural, image, moving, halo, halo_moving, sums, ones, reduced, arrived, notes,
    load_sem, halo_send, halo_recv, band_send, band_recv, note_send, note_recv, mask_in, mask_notes, mask_load, mask_send, mask_recv,
):
    me = lax.axis_index("row")
    count, stride, width = natural.shape
    blocks = width // LANES
    halves = blocks // 8
    band = stride // 2
    node_cols = width // stride

    loads = [
        pltpu.make_async_copy(sections.at[s], natural.at[s], load_sem.at[s])
        for s in range(count)
    ]
    for load in loads:
        load.start()

    mask_copy_in = pltpu.make_async_copy(valid, mask_in, mask_load)
    mask_copy_in.start()

    halo[...] = jnp.zeros(halo.shape, F32)
    arrived[...] = jnp.zeros(arrived.shape, F32)
    notes[...] = jnp.zeros(notes.shape, F32)
    mask_notes[...] = jnp.zeros(mask_notes.shape, F32)
    barrier = pltpu.get_barrier_semaphore()
    offsets = [o for k in range(SPAN, 0, -1) for o in (-k, k)]

    def inside(offset):
        return me >= -offset if offset < 0 else me < rows_of - offset

    for offset in offsets:
        @pl.when(inside(offset))
        def _():
            pl.semaphore_signal(
                barrier, inc=1, device_id={"row": me + offset},
                device_id_type=pl.DeviceIdType.MESH,
            )

    for b in range(2):
        for half in range(halves):
            sums[b, half, TERMS * SHIFTS * 8:, :] = jnp.zeros(
                (sums.shape[2] - TERMS * SHIFTS * 8, LANES), F32
            )
    for t in range(blocks):
        column = lax.broadcasted_iota(jnp.int32, (LANES, LANES), 0) + t * LANES
        lane = lax.broadcasted_iota(jnp.int32, (LANES, LANES), 1)
        node = jnp.where(lane < node_cols, lane, lane - node_cols)
        first = node * stride - stride // 2
        hit = (column >= first) & (column < first + PATCH)
        ones[t * LANES:(t + 1) * LANES, :] = jnp.where(hit, 1.0, 0.0).astype(BF16)

    for s in range(count):
        loads[s].wait()

        @pl.loop(0, stride // 8, unroll=4)
        def _(tile):
            base = pl.multiple_of(tile * 8 * blocks, 8)
            top = pl.multiple_of(tile * 8, 8)
            for t in range(blocks):
                image[s, pl.ds(base + t, 8, stride=blocks), :] = natural[
                    s, pl.ds(top, 8), t * LANES:(t + 1) * LANES
                ]

    size = RADIUS * blocks
    signals = jnp.minimum(me, SPAN) + jnp.minimum(rows_of - 1 - me, SPAN)
    pl.semaphore_wait(barrier, signals)

    def halo_copy(side):
        row = 0 if side == 0 else stride - RADIUS
        start = row * blocks
        return pltpu.make_async_remote_copy(
            src_ref=image.at[1:count, pl.ds(start, size)],
            dst_ref=halo.at[1 - side],
            send_sem=halo_send.at[side],
            recv_sem=halo_recv.at[1 - side],
            device_id={"row": me - 1 if side == 0 else me + 1},
            device_id_type=pl.DeviceIdType.MESH,
        )

    def on_side(side):
        return pl.when(inside(-1 if side == 0 else 1))

    for side in range(2):
        @on_side(side)
        def _():
            halo_copy(side).start()

    npairs = len(PAIRS)

    def row_copy(k, rows, sends, recvs):
        offset = offsets[k]
        return pltpu.make_async_remote_copy(
            src_ref=rows.at[SPAN],
            dst_ref=rows.at[SPAN - offset],
            send_sem=sends.at[k],
            recv_sem=recvs.at[SPAN - offset],
            device_id={"row": me + offset},
            device_id_type=pl.DeviceIdType.MESH,
        )

    mask_copy_in.wait()
    mask = mask_in[:, 0, :].astype(F32)
    mask_notes[SPAN, 0:npairs, 0:node_cols] = mask
    mask_notes[SPAN, 0:npairs, node_cols:2 * node_cols] = mask
    for k, offset in enumerate(offsets):
        @pl.when(inside(offset))
        def _():
            row_copy(k, mask_notes, mask_send, mask_recv).start()

    @pl.loop(0, stride, unroll=16)
    def _(row):
        for s in range(1, count):
            start = pl.multiple_of(row * blocks, 8)
            value = image[s, pl.ds(start, blocks), :]
            for x in range(SHIFTS):
                moving[x, s - 1, row] = shifted(value, x - RADIUS)

    @pl.loop(0, SHIFTS * halves)
    def _(turn):
        x = turn // halves
        half = turn % halves
        sub = pl.multiple_of(half * 8, 8)
        out = pl.multiple_of(x * (TERMS * 8), 8)
        for b in range(2):
            totals = [None] * TERMS
            for y in range(b * band, (b + 1) * band):
                fixed = [
                    image[s, pl.ds(pl.multiple_of(y * blocks + sub, 8), 8), :]
                    for s in range(count - 1)
                ]
                for v in range(SHIFTS):
                    other = y + v - RADIUS
                    if other < 0 or other >= stride:
                        continue
                    moved = [moving[x, s, other, pl.ds(sub, 8), :] for s in range(count - 1)]
                    for p, (first, second) in enumerate(PAIRS):
                        product = fixed[first] * moved[second - 1]
                        i = p * SHIFTS + v
                        totals[i] = product if totals[i] is None else totals[i] + product
            for i in range(TERMS):
                sums[b, half, pl.ds(pl.multiple_of(out + i * 8, 8), 8), :] = totals[i]

    for side in range(2):
        @on_side(side)
        def _():
            pltpu.make_async_copy(halo.at[side], halo.at[side], halo_recv.at[side]).wait()

    for side in range(2):
        @pl.loop(0, RADIUS, unroll=2)
        def _(row):
            for s in range(count - 1):
                value = halo[side, s, pl.ds(pl.multiple_of(row * blocks, 8), blocks), :]
                for x in range(SHIFTS):
                    halo_moving[x, side, s, row] = shifted(value, x - RADIUS)

    @pl.loop(0, SHIFTS * halves, unroll=5)
    def _(turn):
        x = turn // halves
        half = turn % halves
        sub = pl.multiple_of(half * 8, 8)
        out = pl.multiple_of(x * (TERMS * 8), 8)
        for b in range(2):
            totals = {}
            for y in range(b * band, (b + 1) * band):
                for v in range(SHIFTS):
                    other = y + v - RADIUS
                    if 0 <= other < stride:
                        continue
                    row = other + RADIUS if other < 0 else other - stride
                    for p, (first, second) in enumerate(PAIRS):
                        at = pl.multiple_of(y * blocks + sub, 8)
                        product = image[first, pl.ds(at, 8), :] * halo_moving[
                            x, b, second - 1, row, pl.ds(sub, 8), :
                        ]
                        i = p * SHIFTS + v
                        totals[i] = totals[i] + product if i in totals else product
            for i, total in totals.items():
                at = pl.ds(pl.multiple_of(out + i * 8, 8), 8)
                sums[b, half, at, :] = sums[b, half, at, :] + total

    def band_copy(side):
        return pltpu.make_async_remote_copy(
            src_ref=reduced.at[side],
            dst_ref=arrived.at[1 - side],
            send_sem=band_send.at[side],
            recv_sem=band_recv.at[1 - side],
            device_id={"row": me - 1 if side == 0 else me + 1},
            device_id_type=pl.DeviceIdType.MESH,
        )

    first_half = lax.broadcasted_iota(jnp.int32, (LANES // 2, LANES), 1) < node_cols
    total = jnp.zeros((6 * LANES, LANES), F32)
    for t in range(0, blocks, 2):
        wide = jnp.concatenate(
            [
                jnp.concatenate(
                    [sums[b, k // 8, pl.ds(k % 8, LANES, stride=8), :] for k in (t, t + 1)],
                    axis=1,
                )
                for b in range(2)
            ],
            axis=0,
        )
        total = total + jnp.dot(
            jnp.concatenate(thirds(wide), axis=0),
            ones[t * LANES:(t + 2) * LANES, :],
            preferred_element_type=F32,
        )
    total = total[:2 * LANES] + total[2 * LANES:4 * LANES] + total[4 * LANES:]
    for b in range(2):
        part = total[b * LANES:(b + 1) * LANES]
        reduced[b] = jnp.where(first_half, part[:LANES // 2], part[LANES // 2:])

        @on_side(b)
        def _():
            band_copy(b).start()

    term = lax.broadcasted_iota(jnp.int32, (32, LANES), 1)
    line = lax.broadcasted_iota(jnp.int32, (32, LANES), 0)
    shift_x = sum((term >= TERMS * k).astype(jnp.int32) for k in range(1, SHIFTS))
    rest = term - TERMS * shift_x
    pair = sum((rest >= SHIFTS * k).astype(jnp.int32) for k in range(1, len(PAIRS)))
    shift_y = rest - SHIFTS * pair
    kind = (line >= 8).astype(jnp.int32) + (line >= 16).astype(jnp.int32)
    factor = jnp.where(kind == 0, 1, jnp.where(kind == 1, shift_y - RADIUS, shift_x - RADIUS))
    belongs = (pair == line - 8 * kind) & (term < TERMS * SHIFTS) & (line < 24)
    weights_of = jnp.where(belongs, factor, 0).astype(F32).astype(BF16)

    for side in range(2):
        @on_side(side)
        def _():
            pltpu.make_async_copy(
                arrived.at[side], arrived.at[side], band_recv.at[side]
            ).wait()

    corr = (reduced[0] + reduced[1] + arrived[0] + arrived[1]) * (1.0 / PATCH)
    weight = corr * corr + 1.0
    parts = thirds(weight)
    low, high = (
        sum(jnp.dot(half, part, preferred_element_type=F32) for part in parts)
        for half in (weights_of[:, :LANES // 2], weights_of[:, LANES // 2:])
    )
    moments = jnp.where(
        lax.broadcasted_iota(jnp.int32, low.shape, 1) < node_cols, low, high
    )
    moments = moments + pltpu.roll(moments, LANES // 2, 1)
    lane = lax.broadcasted_iota(jnp.int32, (8, LANES), 1)
    line = lax.broadcasted_iota(jnp.int32, (8, LANES), 0)
    denom = jnp.where(line < npairs, moments[0:8], 1.0)
    flow = jnp.where(lane < node_cols, moments[8:16], moments[16:24]) / denom
    notes[SPAN] = flow

    for k, offset in enumerate(offsets):
        @pl.when(inside(offset))
        def _():
            row_copy(k, notes, note_send, note_recv).start()

    for k, offset in enumerate(offsets):
        @pl.when(inside(offset))
        def _():
            slot = SPAN + offset
            pltpu.make_async_copy(
                mask_notes.at[slot], mask_notes.at[slot], mask_recv.at[slot]
            ).wait()
            pltpu.make_async_copy(notes.at[slot], notes.at[slot], note_recv.at[slot]).wait()

    rows_out[0] = notes[...]
    rows_out[1] = mask_notes[...]

    for side in range(2):
        @on_side(side)
        def _():
            halo_copy(side).wait_send()
            band_copy(side).wait_send()
    for k, offset in enumerate(offsets):
        @pl.when(inside(offset))
        def _():
            row_copy(k, mask_notes, mask_send, mask_recv).wait_send()
            row_copy(k, notes, note_send, note_recv).wait_send()


def relax_kernel(rows_of, rows, flows_out, moved_out):
    me = lax.axis_index("row")
    npairs, _, _, node_cols = flows_out.shape
    count = moved_out.shape[0]
    lane = lax.broadcasted_iota(jnp.int32, (8, LANES), 1)
    line = lax.broadcasted_iota(jnp.int32, (8, LANES), 0)
    flow = rows[0, SPAN]
    flows_out[:, 0, 0, :] = flow[:npairs, :node_cols]
    flows_out[:, 1, 0, :] = flow[:npairs, node_cols:]
    node_row = me - SPAN + line
    keep = jnp.where((node_row >= 0) & (node_row < rows_of), 0.1, 0.0)
    at_left = (lane == 0) | (lane == node_cols)
    at_right = (lane == node_cols - 1) | (lane == 2 * node_cols - 1)
    flow_rows = [rows[0, :, p, :] for p in range(npairs)]
    mask_rows = [rows[1, :, p, :] for p in range(npairs)]
    moved = [jnp.zeros((8, LANES), F32) for _ in range(count)]
    for step in range(STEPS):
        grad = [None] * count
        for s in range(1, count):
            d = moved[s]
            left = jnp.where(at_left, 0.0, pltpu.roll(d, 1, 1))
            right = jnp.where(at_right, 0.0, pltpu.roll(d, LANES - 1, 1))
            grad[s] = 4.0 * d - pltpu.roll(d, 1, 0) - pltpu.roll(d, 7, 0) - left - right
        for p, (first, second) in enumerate(PAIRS):
            error = mask_rows[p] * (moved[second] - moved[first] - flow_rows[p])
            grad[second] = grad[second] + error
            if first > 0:
                grad[first] = grad[first] - error
        moved = [moved[0]] + [moved[s] - keep * grad[s] for s in range(1, count)]
    for s in range(count):
        moved_out[s, 0] = moved[s][SPAN:SPAN + 1, :node_cols]
        moved_out[s, 1] = moved[s][SPAN:SPAN + 1, node_cols:]


def local(rows_of, sections, valid):
    count, stride, width = sections.shape
    blocks = width // LANES
    npairs = valid.shape[0]
    node_cols = width // stride
    moving = count - 1
    terms = TERMS * SHIFTS
    rows = pl.pallas_call(
        functools.partial(kernel, rows_of),
        out_shape=jax.ShapeDtypeStruct((2, 8, 8, LANES), F32),
        in_specs=[
            pl.BlockSpec(memory_space=pl.ANY),
            pl.BlockSpec(memory_space=pl.ANY),
        ],
        out_specs=pl.BlockSpec(memory_space=pltpu.VMEM),
        scratch_shapes=[
            pltpu.VMEM((count, stride, width), F32),
            pltpu.VMEM((count, stride * blocks, LANES), F32),
            pltpu.VMEM((SHIFTS, moving, stride, blocks, LANES), F32),
            pltpu.VMEM((2, moving, RADIUS * blocks, LANES), F32),
            pltpu.VMEM((SHIFTS, 2, moving, RADIUS, blocks, LANES), F32),
            pltpu.VMEM((2, blocks // 8, -(-terms // 8) * 64, LANES), F32),
            pltpu.VMEM((width, LANES), BF16),
            pltpu.VMEM((2, LANES // 2, LANES), F32),
            pltpu.VMEM((2, LANES // 2, LANES), F32),
            pltpu.VMEM((8, 8, LANES), F32),
            pltpu.SemaphoreType.DMA((count,)),
            pltpu.SemaphoreType.DMA((2,)),
            pltpu.SemaphoreType.DMA((2,)),
            pltpu.SemaphoreType.DMA((2,)),
            pltpu.SemaphoreType.DMA((2,)),
            pltpu.SemaphoreType.DMA((2 * SPAN,)),
            pltpu.SemaphoreType.DMA((2 * SPAN + 1,)),
            pltpu.VMEM(valid.shape, jnp.int32),
            pltpu.VMEM((8, 8, LANES), F32),
            pltpu.SemaphoreType.DMA,
            pltpu.SemaphoreType.DMA((2 * SPAN,)),
            pltpu.SemaphoreType.DMA((2 * SPAN + 1,)),
        ],
        compiler_params=pltpu.CompilerParams(
            collective_id=0, has_side_effects=True, vmem_limit_bytes=60 * 2**20
        ),
    )(sections, valid)
    return pl.pallas_call(
        functools.partial(relax_kernel, rows_of),
        out_shape=(
            jax.ShapeDtypeStruct((npairs, 2, 1, node_cols), F32),
            jax.ShapeDtypeStruct((count, 2, 1, node_cols), F32),
        ),
        in_specs=[pl.BlockSpec(memory_space=pltpu.VMEM)],
        out_specs=(
            pl.BlockSpec(memory_space=pltpu.VMEM),
            pl.BlockSpec(memory_space=pltpu.VMEM),
        ),
    )(rows)


def solution(mesh):
    return jax.shard_map(
        functools.partial(local, mesh.shape["row"]),
        mesh=mesh,
        in_specs=(P("slab", "row", None), P("slab", "row", None)),
        out_specs=(P("slab", None, "row", None), P("slab", None, "row", None)),
        check_vma=False,
    )
```

```python
import functools

import jax
import jax.numpy as jnp
from jax import lax
from jax.experimental import pallas as pl
from jax.experimental.pallas import tpu as pltpu
from jax.sharding import PartitionSpec as P

PATCH = 64
RADIUS = 2
STEPS = 4
LANES = 128
SPAN = STEPS - 1
PAIRS = ((0, 1), (1, 2), (2, 3), (0, 2), (1, 3))
SHIFTS = 2 * RADIUS + 1
TERMS = len(PAIRS) * SHIFTS
BF16 = jnp.bfloat16
F32 = jnp.float32


def thirds(value):
    high = value.astype(BF16)
    rest = value - high.astype(F32)
    middle = rest.astype(BF16)
    low = (rest - middle.astype(F32)).astype(BF16)
    return high, middle, low


def shifted(row, shift):
    if shift == 0:
        return row
    blocks = row.shape[0]
    lane = lax.broadcasted_iota(jnp.int32, row.shape, 1)
    block = lax.broadcasted_iota(jnp.int32, row.shape, 0)
    if shift > 0:
        other = jnp.where(block == blocks - 1, 0.0, pltpu.roll(row, blocks - 1, 0))
        return pltpu.roll(jnp.where(lane < shift, other, row), LANES - shift, 1)
    other = jnp.where(block == 0, 0.0, pltpu.roll(row, 1, 0))
    return pltpu.roll(jnp.where(lane >= LANES + shift, other, row), -shift, 1)


def kernel(
    rows_of, sections, valid, rows_out,
    natural, image, moving, halo, halo_moving, sums, ones, reduced, arrived, notes,
    load_sem, halo_send, halo_recv, band_send, band_recv, note_send, note_recv, mask_in, mask_notes, mask_load, mask_send, mask_recv,
):
    me = lax.axis_index("row")
    count, stride, width = natural.shape
    blocks = width // LANES
    halves = blocks // 8
    band = stride // 2
    node_cols = width // stride

    loads = [
        pltpu.make_async_copy(sections.at[s], natural.at[s], load_sem.at[s])
        for s in range(count)
    ]
    for load in loads:
        load.start()

    mask_copy_in = pltpu.make_async_copy(valid, mask_in, mask_load)
    mask_copy_in.start()

    halo[...] = jnp.zeros(halo.shape, F32)
    arrived[...] = jnp.zeros(arrived.shape, F32)
    notes[...] = jnp.zeros(notes.shape, F32)
    mask_notes[...] = jnp.zeros(mask_notes.shape, F32)
    barrier = pltpu.get_barrier_semaphore()
    offsets = [o for k in range(SPAN, 0, -1) for o in (-k, k)]

    def inside(offset):
        return me >= -offset if offset < 0 else me < rows_of - offset

    for offset in offsets:
        @pl.when(inside(offset))
        def _():
            pl.semaphore_signal(
                barrier, inc=1, device_id={"row": me + offset},
                device_id_type=pl.DeviceIdType.MESH,
            )

    for b in range(2):
        for half in range(halves):
            sums[b, half, TERMS * SHIFTS * 8:, :] = jnp.zeros(
                (sums.shape[2] - TERMS * SHIFTS * 8, LANES), F32
            )
    for t in range(blocks):
        column = lax.broadcasted_iota(jnp.int32, (LANES, LANES), 0) + t * LANES
        lane = lax.broadcasted_iota(jnp.int32, (LANES, LANES), 1)
        node = jnp.where(lane < node_cols, lane, lane - node_cols)
        first = node * stride - stride // 2
        hit = (column >= first) & (column < first + PATCH)
        ones[t * LANES:(t + 1) * LANES, :] = jnp.where(hit, 1.0, 0.0).astype(BF16)

    for s in range(count):
        loads[s].wait()

        @pl.loop(0, stride // 8, unroll=4)
        def _(tile):
            base = pl.multiple_of(tile * 8 * blocks, 8)
            top = pl.multiple_of(tile * 8, 8)
            for t in range(blocks):
                image[s, pl.ds(base + t, 8, stride=blocks), :] = natural[
                    s, pl.ds(top, 8), t * LANES:(t + 1) * LANES
                ]

    @pl.loop(0, stride // 2, unroll=16)
    def _(row):
        for s in range(1, count):
            start = pl.multiple_of(row * blocks, 8)
            value = image[s, pl.ds(start, blocks), :]
            for x in range(SHIFTS):
                moving[x, s - 1, row] = shifted(value, x - RADIUS)

    size = RADIUS * blocks
    signals = jnp.minimum(me, SPAN) + jnp.minimum(rows_of - 1 - me, SPAN)
    pl.semaphore_wait(barrier, signals)

    def halo_copy(side):
        row = 0 if side == 0 else stride - RADIUS
        start = row * blocks
        return pltpu.make_async_remote_copy(
            src_ref=image.at[1:count, pl.ds(start, size)],
            dst_ref=halo.at[1 - side],
            send_sem=halo_send.at[side],
            recv_sem=halo_recv.at[1 - side],
            device_id={"row": me - 1 if side == 0 else me + 1},
            device_id_type=pl.DeviceIdType.MESH,
        )

    def on_side(side):
        return pl.when(inside(-1 if side == 0 else 1))

    for side in range(2):
        @on_side(side)
        def _():
            halo_copy(side).start()

    npairs = len(PAIRS)

    def row_copy(k, rows, sends, recvs):
        offset = offsets[k]
        return pltpu.make_async_remote_copy(
            src_ref=rows.at[SPAN],
            dst_ref=rows.at[SPAN - offset],
            send_sem=sends.at[k],
            recv_sem=recvs.at[SPAN - offset],
            device_id={"row": me + offset},
            device_id_type=pl.DeviceIdType.MESH,
        )

    @pl.loop(stride // 2, stride, unroll=16)
    def _(row):
        for s in range(1, count):
            start = pl.multiple_of(row * blocks, 8)
            value = image[s, pl.ds(start, blocks), :]
            for x in range(SHIFTS):
                moving[x, s - 1, row] = shifted(value, x - RADIUS)

    @pl.loop(0, SHIFTS * halves)
    def _(turn):
        x = turn // halves
        half = turn % halves
        sub = pl.multiple_of(half * 8, 8)
        out = pl.multiple_of(x * (TERMS * 8), 8)
        for b in range(2):
            totals = [None] * TERMS
            for y in range(b * band, (b + 1) * band):
                fixed = [
                    image[s, pl.ds(pl.multiple_of(y * blocks + sub, 8), 8), :]
                    for s in range(count - 1)
                ]
                for v in range(SHIFTS):
                    other = y + v - RADIUS
                    if other < 0 or other >= stride:
                        continue
                    moved = [moving[x, s, other, pl.ds(sub, 8), :] for s in range(count - 1)]
                    for p, (first, second) in enumerate(PAIRS):
                        product = fixed[first] * moved[second - 1]
                        i = p * SHIFTS + v
                        totals[i] = product if totals[i] is None else totals[i] + product
            for i in range(TERMS):
                sums[b, half, pl.ds(pl.multiple_of(out + i * 8, 8), 8), :] = totals[i]

    mask_copy_in.wait()
    mask = mask_in[:, 0, :].astype(F32)
    mask_notes[SPAN, 0:npairs, 0:node_cols] = mask
    mask_notes[SPAN, 0:npairs, node_cols:2 * node_cols] = mask
    for k, offset in enumerate(offsets):
        @pl.when(inside(offset))
        def _():
            row_copy(k, mask_notes, mask_send, mask_recv).start()

    for side in range(2):
        @on_side(side)
        def _():
            pltpu.make_async_copy(halo.at[side], halo.at[side], halo_recv.at[side]).wait()

    for side in range(2):
        @pl.loop(0, RADIUS, unroll=2)
        def _(row):
            for s in range(count - 1):
                value = halo[side, s, pl.ds(pl.multiple_of(row * blocks, 8), blocks), :]
                for x in range(SHIFTS):
                    halo_moving[x, side, s, row] = shifted(value, x - RADIUS)

    @pl.loop(0, SHIFTS * halves, unroll=5)
    def _(turn):
        x = turn // halves
        half = turn % halves
        sub = pl.multiple_of(half * 8, 8)
        out = pl.multiple_of(x * (TERMS * 8), 8)
        for b in range(2):
            totals = {}
            for y in range(b * band, (b + 1) * band):
                for v in range(SHIFTS):
                    other = y + v - RADIUS
                    if 0 <= other < stride:
                        continue
                    row = other + RADIUS if other < 0 else other - stride
                    for p, (first, second) in enumerate(PAIRS):
                        at = pl.multiple_of(y * blocks + sub, 8)
                        product = image[first, pl.ds(at, 8), :] * halo_moving[
                            x, b, second - 1, row, pl.ds(sub, 8), :
                        ]
                        i = p * SHIFTS + v
                        totals[i] = totals[i] + product if i in totals else product
            for i, total in totals.items():
                at = pl.ds(pl.multiple_of(out + i * 8, 8), 8)
                sums[b, half, at, :] = sums[b, half, at, :] + total

    def band_copy(side):
        return pltpu.make_async_remote_copy(
            src_ref=reduced.at[side],
            dst_ref=arrived.at[1 - side],
            send_sem=band_send.at[side],
            recv_sem=band_recv.at[1 - side],
            device_id={"row": me - 1 if side == 0 else me + 1},
            device_id_type=pl.DeviceIdType.MESH,
        )

    first_half = lax.broadcasted_iota(jnp.int32, (LANES // 2, LANES), 1) < node_cols
    total = jnp.zeros((6 * LANES, LANES), F32)
    for t in range(0, blocks, 2):
        wide = jnp.concatenate(
            [
                jnp.concatenate(
                    [sums[b, k // 8, pl.ds(k % 8, LANES, stride=8), :] for k in (t, t + 1)],
                    axis=1,
                )
                for b in range(2)
            ],
            axis=0,
        )
        total = total + jnp.dot(
            jnp.concatenate(thirds(wide), axis=0),
            ones[t * LANES:(t + 2) * LANES, :],
            preferred_element_type=F32,
        )
    total = total[:2 * LANES] + total[2 * LANES:4 * LANES] + total[4 * LANES:]
    for b in range(2):
        part = total[b * LANES:(b + 1) * LANES]
        reduced[b] = jnp.where(first_half, part[:LANES // 2], part[LANES // 2:])

        @on_side(b)
        def _():
            band_copy(b).start()

    term = lax.broadcasted_iota(jnp.int32, (32, LANES), 1)
    line = lax.broadcasted_iota(jnp.int32, (32, LANES), 0)
    shift_x = sum((term >= TERMS * k).astype(jnp.int32) for k in range(1, SHIFTS))
    rest = term - TERMS * shift_x
    pair = sum((rest >= SHIFTS * k).astype(jnp.int32) for k in range(1, len(PAIRS)))
    shift_y = rest - SHIFTS * pair
    kind = (line >= 8).astype(jnp.int32) + (line >= 16).astype(jnp.int32)
    factor = jnp.where(kind == 0, 1, jnp.where(kind == 1, shift_y - RADIUS, shift_x - RADIUS))
    belongs = (pair == line - 8 * kind) & (term < TERMS * SHIFTS) & (line < 24)
    weights_of = jnp.where(belongs, factor, 0).astype(F32).astype(BF16)

    for side in range(2):
        @on_side(side)
        def _():
            pltpu.make_async_copy(
                arrived.at[side], arrived.at[side], band_recv.at[side]
            ).wait()

    corr = (reduced[0] + reduced[1] + arrived[0] + arrived[1]) * (1.0 / PATCH)
    weight = corr * corr + 1.0
    parts = thirds(weight)
    low, high = (
        sum(jnp.dot(half, part, preferred_element_type=F32) for part in parts)
        for half in (weights_of[:, :LANES // 2], weights_of[:, LANES // 2:])
    )
    moments = jnp.where(
        lax.broadcasted_iota(jnp.int32, low.shape, 1) < node_cols, low, high
    )
    moments = moments + pltpu.roll(moments, LANES // 2, 1)
    lane = lax.broadcasted_iota(jnp.int32, (8, LANES), 1)
    line = lax.broadcasted_iota(jnp.int32, (8, LANES), 0)
    denom = jnp.where(line < npairs, moments[0:8], 1.0)
    flow = jnp.where(lane < node_cols, moments[8:16], moments[16:24]) / denom
    notes[SPAN] = flow

    for k, offset in enumerate(offsets):
        @pl.when(inside(offset))
        def _():
            row_copy(k, notes, note_send, note_recv).start()

    for k, offset in enumerate(offsets):
        @pl.when(inside(offset))
        def _():
            slot = SPAN + offset
            pltpu.make_async_copy(
                mask_notes.at[slot], mask_notes.at[slot], mask_recv.at[slot]
            ).wait()
            pltpu.make_async_copy(notes.at[slot], notes.at[slot], note_recv.at[slot]).wait()

    rows_out[0] = notes[...]
    rows_out[1] = mask_notes[...]

    for side in range(2):
        @on_side(side)
        def _():
            halo_copy(side).wait_send()
            band_copy(side).wait_send()
    for k, offset in enumerate(offsets):
        @pl.when(inside(offset))
        def _():
            row_copy(k, mask_notes, mask_send, mask_recv).wait_send()
            row_copy(k, notes, note_send, note_recv).wait_send()


def relax_kernel(rows_of, rows, flows_out, moved_out):
    me = lax.axis_index("row")
    npairs, _, _, node_cols = flows_out.shape
    count = moved_out.shape[0]
    lane = lax.broadcasted_iota(jnp.int32, (8, LANES), 1)
    line = lax.broadcasted_iota(jnp.int32, (8, LANES), 0)
    flow = rows[0, SPAN]
    flows_out[:, 0, 0, :] = flow[:npairs, :node_cols]
    flows_out[:, 1, 0, :] = flow[:npairs, node_cols:]
    node_row = me - SPAN + line
    keep = jnp.where((node_row >= 0) & (node_row < rows_of), 0.1, 0.0)
    at_left = (lane == 0) | (lane == node_cols)
    at_right = (lane == node_cols - 1) | (lane == 2 * node_cols - 1)
    flow_rows = [rows[0, :, p, :] for p in range(npairs)]
    mask_rows = [rows[1, :, p, :] for p in range(npairs)]
    moved = [jnp.zeros((8, LANES), F32) for _ in range(count)]
    for step in range(STEPS):
        grad = [None] * count
        for s in range(1, count):
            d = moved[s]
            left = jnp.where(at_left, 0.0, pltpu.roll(d, 1, 1))
            right = jnp.where(at_right, 0.0, pltpu.roll(d, LANES - 1, 1))
            grad[s] = 4.0 * d - pltpu.roll(d, 1, 0) - pltpu.roll(d, 7, 0) - left - right
        for p, (first, second) in enumerate(PAIRS):
            error = mask_rows[p] * (moved[second] - moved[first] - flow_rows[p])
            grad[second] = grad[second] + error
            if first > 0:
                grad[first] = grad[first] - error
        moved = [moved[0]] + [moved[s] - keep * grad[s] for s in range(1, count)]
    for s in range(count):
        moved_out[s, 0] = moved[s][SPAN:SPAN + 1, :node_cols]
        moved_out[s, 1] = moved[s][SPAN:SPAN + 1, node_cols:]


def local(rows_of, sections, valid):
    count, stride, width = sections.shape
    blocks = width // LANES
    npairs = valid.shape[0]
    node_cols = width // stride
    moving = count - 1
    terms = TERMS * SHIFTS
    rows = pl.pallas_call(
        functools.partial(kernel, rows_of),
        out_shape=jax.ShapeDtypeStruct((2, 8, 8, LANES), F32),
        in_specs=[
            pl.BlockSpec(memory_space=pl.ANY),
            pl.BlockSpec(memory_space=pl.ANY),
        ],
        out_specs=pl.BlockSpec(memory_space=pltpu.VMEM),
        scratch_shapes=[
            pltpu.VMEM((count, stride, width), F32),
            pltpu.VMEM((count, stride * blocks, LANES), F32),
            pltpu.VMEM((SHIFTS, moving, stride, blocks, LANES), F32),
            pltpu.VMEM((2, moving, RADIUS * blocks, LANES), F32),
            pltpu.VMEM((SHIFTS, 2, moving, RADIUS, blocks, LANES), F32),
            pltpu.VMEM((2, blocks // 8, -(-terms // 8) * 64, LANES), F32),
            pltpu.VMEM((width, LANES), BF16),
            pltpu.VMEM((2, LANES // 2, LANES), F32),
            pltpu.VMEM((2, LANES // 2, LANES), F32),
            pltpu.VMEM((8, 8, LANES), F32),
            pltpu.SemaphoreType.DMA((count,)),
            pltpu.SemaphoreType.DMA((2,)),
            pltpu.SemaphoreType.DMA((2,)),
            pltpu.SemaphoreType.DMA((2,)),
            pltpu.SemaphoreType.DMA((2,)),
            pltpu.SemaphoreType.DMA((2 * SPAN,)),
            pltpu.SemaphoreType.DMA((2 * SPAN + 1,)),
            pltpu.VMEM(valid.shape, jnp.int32),
            pltpu.VMEM((8, 8, LANES), F32),
            pltpu.SemaphoreType.DMA,
            pltpu.SemaphoreType.DMA((2 * SPAN,)),
            pltpu.SemaphoreType.DMA((2 * SPAN + 1,)),
        ],
        compiler_params=pltpu.CompilerParams(
            collective_id=0, has_side_effects=True, vmem_limit_bytes=60 * 2**20
        ),
    )(sections, valid)
    return pl.pallas_call(
        functools.partial(relax_kernel, rows_of),
        out_shape=(
            jax.ShapeDtypeStruct((npairs, 2, 1, node_cols), F32),
            jax.ShapeDtypeStruct((count, 2, 1, node_cols), F32),
        ),
        in_specs=[pl.BlockSpec(memory_space=pltpu.VMEM)],
        out_specs=(
            pl.BlockSpec(memory_space=pltpu.VMEM),
            pl.BlockSpec(memory_space=pltpu.VMEM),
        ),
    )(rows)


def solution(mesh):
    return jax.shard_map(
        functools.partial(local, mesh.shape["row"]),
        mesh=mesh,
        in_specs=(P("slab", "row", None), P("slab", "row", None)),
        out_specs=(P("slab", None, "row", None), P("slab", None, "row", None)),
        check_vma=False,
    )
```
